512 devices in a mesh: basin: 8 (over x, core), front: 64 (over y, z).
Axes of the slice: x: 4, y: 4, z: 16, core: 2. Of those that a mesh axis runs over, the one named last changes fastest.
Arguments:
- right_side: float32 [4, 8, 128, 512], P(None, 'basin', 'front'), may hold values from -8 to 8
- offsets: float32 [2, 8, 128, 512], P(None, 'basin', 'front'), may hold values from 0 to 1
- counts: int32 [8, 128], P('basin', 'front'), may hold values from 128 to 512, as said below
Outputs:
- solution_field: float32 [4, 8, 128, 512], P(None, 'basin', 'front')
- residual: float32 [4, 8, 128, 512], P(None, 'basin', 'front')
The draws below stay inside these ranges and needn't reach their ends.
Inputs may be any that keep to these rules, and one draw needn't show every extreme that they name: Points p < counts of a block are live, the others are padding. Some block holds 512 live points, some 512 // 4.
All inputs are finite; a program needn't handle non-finite values.
Results may differ from the reference program's by a relative error of at most 0.0003.
Values sent between devices are 32-bit elements; how exact they have to be, the bound alone decides.
A program may use at most 64 MiB of HBM per device.

```python
import jax
import jax.numpy as jnp
from jax import lax

P_SIZE = 512
F = 4
ITERS = 3
NBX = 8
NBY = 128


def draw_counts(key, part):
    key = jax.random.fold_in(key, 7)
    values = jax.random.randint(key, (NBX, NBY), P_SIZE // 4, P_SIZE + 1)
    values = values.at[0, 0].set(P_SIZE).at[NBX - 1, NBY - 1].set(P_SIZE // 4)
    return values.astype(jnp.int32)


def levels(own_key, dims, split, low, high):
    loudness, own = 1.0, jax.random.fold_in(own_key, 6)
    for dim, blocks in split:
        draws = jnp.exp(jax.random.uniform(jax.random.fold_in(own, dim), (blocks,), jnp.float32, low / len(split), high / len(split)))
        loudness = loudness * jnp.repeat(draws, dims[dim] // blocks).reshape([-1 if axis == dim else 1 for axis in range(len(dims))])
    return loudness


def scatter_about(own_key, dims, scale, reach, shards=(), kind=jnp.bfloat16):
    loudness = levels(own_key, dims, shards, -0.22, 0.18) if shards else 1.0
    array = jax.random.normal(own_key, dims, jnp.float32) * scale * loudness
    return jnp.minimum(jnp.maximum(array, -reach), reach).astype(kind)


def setup_inputs(seed: int = 0) -> dict:
    splits = jax.random.split(jax.random.key(seed), 4)
    right_side = scatter_about(splits[0], (F, NBX, NBY, P_SIZE), 1.0, 8.0, ((1, 8), (2, 64)), jnp.float32)
    offsets = jnp.clip(1.0 * jax.random.uniform(splits[1], (2, NBX, NBY, P_SIZE), jnp.float32) ** levels(splits[1], (2, NBX, NBY, P_SIZE), ((1, 8), (2, 64)), -0.2, 0.2), 0.0, 1.0)
    counts = draw_counts(jax.random.fold_in(splits[3], 71), 0)
    return dict(right_side=right_side, offsets=offsets, counts=counts)


ridge = 0.25
neighbors = [(-1, -1), (-1, 0), (-1, 1), (0, -1), (0, 0), (0, 1), (1, -1), (1, 0), (1, 1)]

def wendland(delta_x, delta_y):
    radius = jnp.sqrt(delta_x * delta_x + delta_y * delta_y)
    near = jnp.maximum(1.0 - radius, 0.0)
    near_sq = near * near
    return near_sq * near_sq * (4.0 * radius + 1.0)

def operate(direction, offsets, live):
    coef_pad = jnp.pad(direction, ((0, 0), (1, 1), (1, 1), (0, 0)))
    offs_pad = jnp.pad(offsets, ((0, 0), (1, 1), (1, 1), (0, 0)))

    def row_image(row_index):
        centre = lax.dynamic_slice_in_dim(offs_pad, row_index + 1, 1, 1)[:, 0, 1:1 + NBY]
        total = jnp.zeros((F, NBY, P_SIZE), jnp.float32)
        for row_step, col_step in neighbors:
            other_offs = lax.dynamic_slice_in_dim(offs_pad, row_index + 1 + row_step, 1, 1)[:, 0, 1 + col_step:1 + col_step + NBY]
            other_coef = lax.dynamic_slice_in_dim(coef_pad, row_index + 1 + row_step, 1, 1)[:, 0, 1 + col_step:1 + col_step + NBY]
            delta_x = centre[0][:, :, None] - other_offs[0][:, None, :] - float(row_step)
            delta_y = centre[1][:, :, None] - other_offs[1][:, None, :] - float(col_step)
            kernel = wendland(delta_x, delta_y)
            total = total + jnp.einsum('bij,fbj->fbi', kernel, other_coef, precision=lax.Precision.HIGHEST)
        return total
    rows = lax.map(row_image, jnp.arange(NBX, dtype=jnp.int32))
    summed = jnp.transpose(rows, (1, 0, 2, 3))
    return ridge * direction + live * (summed / P_SIZE)

def reference(right_side, offsets, counts):
    live = (lax.broadcasted_iota(jnp.int32, (NBX, NBY, P_SIZE), 2) < counts[:, :, None]).astype(jnp.float32)
    residual = right_side * live
    solution_field = jnp.zeros_like(residual)
    direction = residual
    norm_now = lax.optimization_barrier(jnp.sum(residual * residual, axis=(1, 2, 3)))
    for repeat in range(ITERS):
        image = operate(direction, offsets, live)
        alpha = norm_now / lax.optimization_barrier(jnp.sum(direction * image, axis=(1, 2, 3)))
        solution_field = solution_field + alpha[:, None, None, None] * direction
        residual = residual - alpha[:, None, None, None] * image
        norm_next = lax.optimization_barrier(jnp.sum(residual * residual, axis=(1, 2, 3)))
        direction = residual + (norm_next / norm_now)[:, None, None, None] * direction
        norm_now = norm_next
    return (solution_field, residual)
```

```python
import jax
import jax.numpy as jnp
from jax import lax
from jax.experimental import pallas as pl
from jax.experimental.pallas import tpu as pltpu
from jax.sharding import PartitionSpec as P

MESH = pl.DeviceIdType.MESH
F32, BF16 = jnp.float32, jnp.bfloat16
STEPS = 3
FIELDS = 4
POINTS = 512
RIDGE = 0.25
CHUNK = 256
Z_SIZE = 16

SIDES = ((1, 0), (-1, 0), (0, 1), (0, -1), (1, 1), (1, -1), (-1, 1), (-1, -1))


def wrap(value, count):
    return lax.rem(value + count, count)


def halves(kernel_values):
    high = kernel_values.astype(BF16)
    return high, (kernel_values - high.astype(F32)).astype(BF16)


def left_operand(vector):
    high = vector.astype(BF16).astype(F32)
    stacked = jnp.concatenate([high, vector - high, jnp.zeros((8, POINTS), F32)], axis=0)
    return stacked.astype(BF16)


def times(left, high, low):
    return jnp.dot(left, high, preferred_element_type=F32) + jnp.dot(left, low, preferred_element_type=F32)


def quarter_wendland(distance_sq):
    radius = pltpu.reciprocal(lax.rsqrt(distance_sq), approx=True)
    near = jnp.maximum(1.0 - radius, 0.0)
    near_sq = near * near
    return near_sq * near_sq * (radius + 0.25)


def joined(top, bottom):
    return jnp.concatenate([top[0:4] + top[4:8], bottom[0:4] + bottom[4:8]], axis=0)


def fold(values):
    part = values[:, 0:128]
    for lane in range(128, POINTS, 128):
        part = part + values[:, lane : lane + 128]
    return part[0:4] + part[4:8]


def kernel(
    sizes, right_ref, offs_ref, counts_ref, out_ref, res_ref,
    first, second, third, high, low, part, got_basin, got_z, got_y,
    halo_send, halo_recv, sum_send, sum_recv,
):
    n_basin, n_front, n_y, n_z = sizes
    basin, front = lax.axis_index("basin"), lax.axis_index("front")
    y_at, z_at = front // n_z, lax.rem(front, n_z)

    def basin_peer(step):
        return (wrap(basin + step, n_basin), front)

    def z_peer(step):
        return (basin, y_at * n_z + wrap(z_at + step, n_z))

    def y_peer(step):
        return (basin, wrap(y_at + step, n_y) * n_z + z_at)

    def side_peer(side):
        return (wrap(basin + side[0], n_basin), wrap(front + side[1], n_front))

    groups = ((basin_peer, n_basin, got_basin), (z_peer, n_z, got_z), (y_peer, n_y, got_y))

    barrier = pltpu.get_barrier_semaphore()
    greeted = [peer(step) for peer, count, _ in groups for step in range(1, count)]
    greeted += [side_peer(side) for side in SIDES if side[1] != 0]
    for device in greeted:
        pl.semaphore_signal(barrier, inc=1, device_id=device, device_id_type=MESH)

    lane = lax.broadcasted_iota(jnp.int32, (FIELDS, POINTS), 1)
    alive = [(lane < counts_ref[0, block]).astype(F32) for block in range(2)]
    live = jnp.concatenate(alive, axis=0)
    residual = []
    for block in range(2):
        field = right_ref[:, 0, block, :] * alive[block]
        residual.append(field)
        first[5 + block] = jnp.concatenate(
            [field, offs_ref[:, 0, block, :], jnp.zeros((2, POINTS), F32)], axis=0
        )
    residual = jnp.concatenate(residual, axis=0)

    pl.semaphore_wait(barrier, len(greeted))

    def halo_copy(buffer, turn, index):
        row, col = SIDES[index]
        target = 1 - row
        if col == 0:
            source, dest = pl.ds(5, 2), pl.ds(4 * target + 1, 2)
        elif col == 1:
            source, dest = pl.ds(6, 1), pl.ds(4 * target, 1)
        else:
            source, dest = pl.ds(5, 1), pl.ds(4 * target + 3, 1)
        return pltpu.make_async_remote_copy(
            src_ref=buffer.at[source], dst_ref=buffer.at[dest],
            send_sem=halo_send.at[turn, index], recv_sem=halo_recv.at[turn, index],
            device_id=side_peer(SIDES[index]), device_id_type=MESH,
        )

    def halo_start(buffer, turn):
        copies = [halo_copy(buffer, turn, index) for index in range(8)]
        for copy in copies:
            copy.start()
        return copies

    copies = halo_start(first, 0)

    arrivals = {0: (0, (4, 5)), 1: (None, (2, 3)), 2: (1, (6, 7))}

    def far(row, col):
        outside = jnp.float32(0.0)
        if row == 0:
            outside = outside + (basin == 0).astype(F32)
        if row == 2:
            outside = outside + (basin == n_basin - 1).astype(F32)
        if col == 0:
            outside = outside + (front == 0).astype(F32)
        if col == 3:
            outside = outside + (front == n_front - 1).astype(F32)
        return outside * 64.0

    own_x = [first[5 + block, 4:5, :] for block in range(2)]
    own_y = [first[5, 5:6, :], first[6, 5:6, :] + 1.0]

    def users(col):
        return [block for block in range(2) if 0 <= col - block <= 2]

    def slot(block, row, col):
        return 9 * block + 3 * row + col - block

    zero = jnp.zeros((16, POINTS), F32)

    def build(row, cols, sums):
        for col in cols:
            packed = first[4 * row + col]
            columns = jnp.transpose(packed)
            at_x = columns[:, 4:5] + (float(row - 1) + far(row, col))
            at_y = columns[:, 5:6] + float(col - 1)
            left = left_operand(packed[0:4])
            for begin in range(0, POINTS, CHUNK):
                rows = slice(begin, begin + CHUNK)
                for block in users(col):
                    delta_x = own_x[block] - at_x[rows]
                    delta_y = own_y[block] - at_y[rows]
                    top, rest = halves(quarter_wendland(delta_x * delta_x + delta_y * delta_y))
                    place = slot(block, row, col)
                    high[place, rows, :] = top
                    low[place, rows, :] = rest
                    sums[block] = sums[block] + times(left[:, rows], top, rest)
        return sums

    def use(buffer, row, cols, sums):
        for col in cols:
            left = left_operand(buffer[4 * row + col])
            for block in users(col):
                place = slot(block, row, col)
                sums[block] = sums[block] + times(left, high[place], low[place])
        return sums

    def product(work, copies, between):
        sums = [zero, zero]
        for row in (1, 0, 2):
            middle, outer = arrivals[row]
            if middle is not None:
                copies[middle].wait_recv()
            sums = work(row, (1, 2), sums)
            for index in outer:
                copies[index].wait_recv()
            sums = work(row, (0, 3), sums)
            between(row)
        return joined(*sums) * (live * (4.0 / POINTS))

    def stage_all(turn, stage):
        got = groups[stage][2]
        return pltpu.make_async_remote_copy(
            src_ref=got.at[turn], dst_ref=got.at[turn],
            send_sem=sum_send.at[turn, stage], recv_sem=sum_recv.at[turn, stage],
            device_id=groups[stage][0](1), device_id_type=MESH,
        )

    def stage_start(turn, stage, value):
        part[turn, stage] = value
        peer, count, got = groups[stage]
        for step in range(1, count):
            pltpu.make_async_remote_copy(
                src_ref=part.at[turn, stage], dst_ref=got.at[turn, step - 1],
                send_sem=sum_send.at[turn, stage], recv_sem=sum_recv.at[turn, stage],
                device_id=peer(step), device_id_type=MESH,
            ).start()

    def stage_end(turn, stage):
        stage_all(turn, stage).wait_recv()
        return part[turn, stage] + jnp.sum(groups[stage][2][turn], axis=0)

    def sum_start(turn, residual, image):
        stage_start(
            turn, 0,
            jnp.concatenate([fold(residual * residual), fold(residual * image)], axis=0),
        )

    def sum_step(turn, stage):
        stage_start(turn, stage + 1, stage_end(turn, stage))

    def sum_end(turn):
        total = jnp.sum(stage_end(turn, 2), axis=1, keepdims=True)
        norm, curve = total[0:4], total[4:8]
        return jnp.concatenate([norm, norm], axis=0), jnp.concatenate([curve, curve], axis=0)

    buffers = (first, second, third)
    image = product(build, copies, lambda row: None)
    all_copies = [copies]
    found = jnp.zeros((2 * FIELDS, POINTS), F32)
    for turn in range(STEPS):
        last = turn == STEPS - 1
        if not last:
            buffer = buffers[turn + 1]
            buffer[5] = image[0:4]
            buffer[6] = image[4:8]
            copies = halo_start(buffer, turn + 1)
            all_copies.append(copies)
        sum_start(turn, residual, image)
        if not last:

            def between(row, turn=turn):
                if row == 1:
                    sum_step(turn, 0)
                if row == 0:
                    sum_step(turn, 1)

            image_next = product(lambda row, cols, sums: use(buffer, row, cols, sums), copies, between)
        else:
            sum_step(turn, 0)
            sum_step(turn, 1)
        norm, curve = sum_end(turn)
        curve = RIDGE * norm + curve
        if turn == 0:
            alpha = norm / curve
            direction, mapped = residual, image
            if not last:
                mapped_twice = image_next
        else:
            beta = norm / norm_before
            alpha = norm / (curve - beta * norm / alpha)
            direction = residual + beta * direction
            mapped = image + beta * mapped
            if not last:
                mapped_twice = image_next + beta * mapped_twice
        found = found + alpha * direction
        residual = residual - alpha * (RIDGE * direction + mapped)
        if not last:
            image = image - alpha * (RIDGE * mapped + mapped_twice)
        norm_before = norm

    for block in range(2):
        out_ref[:, 0, block, :] = found[4 * block : 4 * block + 4]
        res_ref[:, 0, block, :] = residual[4 * block : 4 * block + 4]

    for copies in all_copies:
        for copy in copies:
            copy.wait_send()
    for turn in range(STEPS):
        for stage in range(3):
            stage_all(turn, stage).wait_send()


def solution(mesh):
    n_basin, n_front = mesh.shape["basin"], mesh.shape["front"]
    n_z = Z_SIZE
    sizes = (n_basin, n_front, n_front // n_z, n_z)

    def step(right_side, offsets, counts):
        shape = jax.ShapeDtypeStruct(right_side.shape, F32)
        return pl.pallas_call(
            lambda *refs: kernel(sizes, *refs),
            out_shape=(shape, shape),
            in_specs=[
                pl.BlockSpec(memory_space=pltpu.VMEM),
                pl.BlockSpec(memory_space=pltpu.VMEM),
                pl.BlockSpec(memory_space=pltpu.SMEM),
            ],
            out_specs=(pl.BlockSpec(memory_space=pltpu.VMEM), pl.BlockSpec(memory_space=pltpu.VMEM)),
            scratch_shapes=[
                pltpu.VMEM((12, 8, POINTS), F32),
                pltpu.VMEM((12, FIELDS, POINTS), F32),
                pltpu.VMEM((12, FIELDS, POINTS), F32),
                pltpu.VMEM((18, POINTS, POINTS), BF16),
                pltpu.VMEM((18, POINTS, POINTS), BF16),
                pltpu.VMEM((STEPS, 3, 8, 128), F32),
                pltpu.VMEM((STEPS, n_basin - 1, 8, 128), F32),
                pltpu.VMEM((STEPS, n_z - 1, 8, 128), F32),
                pltpu.VMEM((STEPS, n_front // n_z - 1, 8, 128), F32),
                pltpu.SemaphoreType.DMA((STEPS, 8)),
                pltpu.SemaphoreType.DMA((STEPS, 8)),
                pltpu.SemaphoreType.DMA((STEPS, 3)),
                pltpu.SemaphoreType.DMA((STEPS, 3)),
            ],
            compiler_params=pltpu.CompilerParams(
                collective_id=0, has_side_effects=True, vmem_limit_bytes=48 * 2**20
            ),
        )(right_side, offsets, counts)

    part = P(None, "basin", "front", None)
    return jax.shard_map(
        step, mesh=mesh, in_specs=(part, part, P("basin", "front")), out_specs=(part, part), check_vma=False
    )
```

```python
import jax
import jax.numpy as jnp
from jax import lax
from jax.experimental import pallas as pl
from jax.experimental.pallas import tpu as pltpu
from jax.sharding import PartitionSpec as P

MESH = pl.DeviceIdType.MESH
F32, BF16 = jnp.float32, jnp.bfloat16
FIELDS = 4
POINTS = 512
RIDGE = 0.25
CHUNK = 256
Z_SIZE = 16

SIDES = ((1, 0), (-1, 0), (0, 1), (0, -1), (1, 1), (1, -1), (-1, 1), (-1, -1))
ARRIVALS = ((0, (1, 2)), (2, (1, 2)), (1, (0,)), (1, (3,)), (0, (0,)), (0, (3,)), (2, (0,)), (2, (3,)))
ORDER = (0, 2, 4, 5, 1, 3, 6, 7)
SEND_ORDER = (4, 5, 0, 2, 6, 7, 1, 3)


def wrap(value, count):
    return lax.rem(value + count, count)


def halves(kernel_values):
    high = kernel_values.astype(BF16)
    return high, (kernel_values - high.astype(F32)).astype(BF16)


def left_operand(vector):
    high = vector.astype(BF16).astype(F32)
    rest = vector - high
    middle = rest.astype(BF16).astype(F32)
    stacked = jnp.concatenate([high, middle, rest - middle, jnp.zeros((4, POINTS), F32)], axis=0)
    return stacked.astype(BF16)


def times(left, high, low):
    return jnp.dot(left, high, preferred_element_type=F32) + jnp.dot(left, low, preferred_element_type=F32)


def quarter_wendland(distance_sq):
    radius = pltpu.reciprocal(lax.rsqrt(distance_sq), approx=True)
    near = jnp.maximum(1.0 - radius, 0.0)
    near_sq = near * near
    return near_sq * near_sq * (radius + 0.25)


def two_sum(a, b):
    total = a + b
    other = total - a
    return total, (a - (total - other)) + (b - other)


def quick_sum(a, b):
    total = a + b
    return total, b - (total - a)


def split(a):
    scaled = a * 4097.0
    high = scaled - (scaled - a)
    return high, a - high


def two_product(a, b):
    total = a * b
    a_high, a_low = split(a)
    b_high, b_low = split(b)
    return total, ((a_high * b_high - total) + a_high * b_low + a_low * b_high) + a_low * b_low


def minus(a, b):
    total, rest = two_sum(a[0], -b[0])
    return quick_sum(total, rest + (a[1] - b[1]))


def product_of(a, b):
    total, rest = two_product(a[0], b[0])
    return quick_sum(total, rest + (a[0] * b[1] + a[1] * b[0]))


def ratio(a, b):
    first = a[0] / b[0]
    left = minus(a, product_of(b, (first, jnp.zeros_like(first))))
    return quick_sum(first, (left[0] + left[1]) / b[0])


def coefficients(moments):
    a0 = ratio(moments[1], moments[0])
    one = [None] + [minus(moments[k + 1], product_of(a0, moments[k])) for k in range(1, 5)]
    mean_one = ratio(one[2], one[1])
    a1 = minus(mean_one, a0)
    b1 = ratio(one[1], moments[0])
    two = [
        minus(minus(one[k + 1], product_of(a1, one[k])), product_of(b1, moments[k])) for k in (2, 3)
    ]
    a2 = two[1][0] / two[0][0] - mean_one[0]
    b2 = two[0][0] / one[1][0]
    a0, a1, b1 = a0[0], a1[0], b1[0]
    constant, linear = a0 * a1 - b1, -(a0 + a1)
    c2, c1, c0 = linear - a2, constant - a2 * linear - b2, b2 * a0 - a2 * constant
    at_ridge = ((c2 - RIDGE) * -RIDGE + c1) * -RIDGE + c0
    d3 = 1.0 / at_ridge
    d2, d1, d0 = c2 * d3, c1 * d3, c0 * d3
    x2 = -d3
    x1 = -d2 - RIDGE * x2
    x0 = -d1 - RIDGE * x1
    return (x0, x1, x2), (d0, d1, d2, d3)


def joined(top, bottom):
    return jnp.concatenate([x[0:4] + (x[4:8] + x[8:12]) for x in (top, bottom)], axis=0)


def fold(values):
    part = values[:, 0:128]
    for lane in range(128, POINTS, 128):
        part = part + values[:, lane : lane + 128]
    return part[0:4] + part[4:8]


def kernel(
    sizes, right_hbm, offs_hbm, counts_hbm, out_ref, res_ref,
    right_ref, offs_ref, counts_ref, first, second, third, high, low, part, got_core, got_xy, got_z,
    load_sem, halo_send, halo_recv, sum_send, sum_recv,
):
    n_x, n_y, n_z = sizes
    n_basin, n_front = 2 * n_x, n_y * n_z
    basin, front = lax.axis_index("basin"), lax.axis_index("front")
    x_at, core_at = basin // 2, lax.rem(basin, 2)
    y_at, z_at = front // n_z, lax.rem(front, n_z)

    loads = [
        pltpu.make_async_copy(source, dest, load_sem.at[index])
        for index, (source, dest) in enumerate(
            ((right_hbm, right_ref), (offs_hbm, offs_ref), (counts_hbm, counts_ref))
        )
    ]
    for load in loads:
        load.start()

    def hops(step, count):
        return min(step, count - step)

    def xy_peer(step_x, step_y):
        return (2 * wrap(x_at + step_x, n_x) + core_at, wrap(y_at + step_y, n_y) * n_z + z_at)

    def side_peer(side):
        return (wrap(basin + side[0], n_basin), wrap(front + side[1], n_front))

    xy_steps = [(x, y) for x in range(n_x) for y in range(n_y) if x or y]
    xy_steps.sort(key=lambda step: -hops(step[0], n_x) - hops(step[1], n_y))
    z_steps = sorted(range(1, n_z), key=lambda step: -hops(step, n_z))
    stages = (
        ([(2 * x_at + 1 - core_at, front)], got_core),
        ([xy_peer(*step) for step in xy_steps], got_xy),
        ([(basin, y_at * n_z + wrap(z_at + step, n_z)) for step in z_steps], got_z),
    )

    barrier = pltpu.get_barrier_semaphore()
    greeted = [side_peer(side) for side in SIDES]
    for peers, _ in stages:
        greeted += peers
    for device in greeted:
        pl.semaphore_signal(barrier, inc=1, device_id=device, device_id_type=MESH)

    for load in loads:
        load.wait()
    lane = lax.broadcasted_iota(jnp.int32, (FIELDS, POINTS), 1)
    alive, residual = [], []
    for block in range(2):
        alive.append((lane < counts_ref[0:1, block : block + 1]).astype(F32))
        field = right_ref[:, 0, block, :] * alive[block]
        residual.append(field)
        first[5 + block] = jnp.concatenate(
            [field, offs_ref[:, 0, block, :], jnp.zeros((2, POINTS), F32)], axis=0
        )
    scale = jnp.concatenate(alive, axis=0) * (4.0 / POINTS)
    residual = jnp.concatenate(residual, axis=0)

    pl.semaphore_wait(barrier, len(greeted))

    def halo_start(buffer, turn):
        copies = []
        for index, (row, col) in enumerate(SIDES):
            target = 1 - row
            if col == 0:
                source, dest = pl.ds(5, 2), pl.ds(4 * target + 1, 2)
            elif col == 1:
                source, dest = pl.ds(6, 1), pl.ds(4 * target, 1)
            else:
                source, dest = pl.ds(5, 1), pl.ds(4 * target + 3, 1)
            copies.append(
                pltpu.make_async_remote_copy(
                    src_ref=buffer.at[source], dst_ref=buffer.at[dest],
                    send_sem=halo_send.at[turn, index], recv_sem=halo_recv.at[turn, index],
                    device_id=side_peer((row, col)), device_id_type=MESH,
                )
            )
        for index in SEND_ORDER:
            copies[index].start()
        return copies

    def far(row, col):
        outside = jnp.float32(0.0)
        if row == 0:
            outside = outside + (basin == 0).astype(F32)
        if row == 2:
            outside = outside + (basin == n_basin - 1).astype(F32)
        if col == 0:
            outside = outside + (front == 0).astype(F32)
        if col == 3:
            outside = outside + (front == n_front - 1).astype(F32)
        return outside * 64.0

    def users(col):
        return [block for block in range(2) if 0 <= col - block <= 2]

    def slot(block, row, col):
        return 9 * block + 3 * row + col - block

    zero = jnp.zeros((16, POINTS), F32)

    def build(row, cols, sums):
        sums = list(sums)
        for col in cols:
            packed = first[4 * row + col]
            columns = jnp.transpose(packed)
            at_x = columns[:, 4:5] + (float(row - 1) + far(row, col))
            at_y = columns[:, 5:6] + float(col - 1)
            left = left_operand(packed[0:4])
            for begin in range(0, POINTS, CHUNK):
                rows = slice(begin, begin + CHUNK)
                for block in users(col):
                    delta_x = own_x[block] - at_x[rows]
                    delta_y = own_y[block] - at_y[rows]
                    top, rest = halves(quarter_wendland(delta_x * delta_x + delta_y * delta_y))
                    place = slot(block, row, col)
                    high[place, rows, :] = top
                    low[place, rows, :] = rest
                    sums[block] = sums[block] + times(left[:, rows], top, rest)
        return sums

    def use(buffer, row, cols, sums):
        sums = list(sums)
        for col in cols:
            left = left_operand(buffer[4 * row + col])
            for block in users(col):
                place = slot(block, row, col)
                sums[block] = sums[block] + times(left, high[place], low[place])
        return sums

    def gather(work, copies, indices, sums):
        for index in indices:
            copies[index].wait_recv()
            sums = work(*ARRIVALS[index], sums)
        return sums

    row_at = lax.broadcasted_iota(jnp.int32, (8, 128), 0)
    lane_at = lax.broadcasted_iota(jnp.int32, (8, 128), 1)

    def own_moment(order, a, b):
        total = jnp.sum(fold(a * b), axis=1, keepdims=True)
        return jnp.where(lane_at[0:4] == row_at[0:4] + FIELDS * order, total, 0.0)

    def sum_copy(stage, index, peer):
        got = stages[stage][1]
        return pltpu.make_async_remote_copy(
            src_ref=part.at[pl.ds(stage, 1)], dst_ref=got.at[pl.ds(index, 1)],
            send_sem=sum_send.at[stage], recv_sem=sum_recv.at[stage],
            device_id=peer, device_id_type=MESH,
        )

    def sum_all(stage):
        peers, got = stages[stage]
        return pltpu.make_async_remote_copy(
            src_ref=got.at[pl.ds(0, len(peers))], dst_ref=got.at[pl.ds(0, len(peers))],
            send_sem=sum_send.at[stage], recv_sem=sum_recv.at[stage],
            device_id=peers[0], device_id_type=MESH,
        )

    def sum_start(stage, total, rest):
        peers, got = stages[stage]
        row = total if rest is None else jnp.where(lane_at[0:1] < 64, total, pltpu.roll(rest, 64, 1))
        part[stage : stage + 1] = row
        for index, peer in enumerate(peers):
            sum_copy(stage, index, peer).start()
        got[len(peers) : len(peers) + 1] = row

    def sum_end(stage):
        peers, got = stages[stage]
        sum_all(stage).wait_recv()
        count = len(peers) + 1
        if count < 8:
            total, rest = got[0:1], jnp.zeros((1, 128), F32)
            for index in range(1, count):
                total, more = two_sum(total, got[index : index + 1])
                rest = rest + more
        else:
            total, rest = got[0:8], jnp.zeros((8, 128), F32)
            for begin in range(8, count, 8):
                total, more = two_sum(total, got[begin : begin + 8])
                rest = rest + more
            for step in (4, 2, 1):
                total, more = two_sum(total, pltpu.roll(total, step, 0))
                rest = rest + pltpu.roll(rest, step, 0) + more
            total, rest = total[0:1], rest[0:1]
        return total, rest + pltpu.roll(total, 64, 1)

    copies = halo_start(first, 0)
    all_copies = [copies]
    own_x = [first[5 + block, 4:5, :] for block in range(2)]
    own_y = [first[5, 5:6, :], first[6, 5:6, :] + 1.0]
    sums = build(1, (1, 2), [zero, zero])
    sums = gather(build, copies, ORDER, sums)
    powers = [residual, joined(*sums) * scale]

    def send(buffer, turn):
        buffer[5] = powers[-1][0:4]
        buffer[6] = powers[-1][4:8]
        all_copies.append(halo_start(buffer, turn))
        return all_copies[-1], lambda row, cols, sums: use(buffer, row, cols, sums)

    copies, work = send(second, 1)
    moments = own_moment(0, powers[0], powers[0]) + own_moment(1, powers[0], powers[1])
    moments = moments + own_moment(2, powers[1], powers[1])
    sums = work(1, (1, 2), [zero, zero])
    sums = gather(work, copies, ORDER, sums)
    powers.append(joined(*sums) * scale)

    copies, work = send(third, 2)
    moments = moments + own_moment(3, powers[1], powers[2]) + own_moment(4, powers[2], powers[2])
    own = work(1, (1, 2), [zero, zero])
    sums = gather(work, copies, ORDER[:4], [zero, zero])
    half = joined(*[a + 2.0 * b for a, b in zip(own, sums)]) * scale
    moments = jnp.sum(moments + own_moment(5, powers[2], half), axis=0, keepdims=True)
    sum_start(0, moments, None)
    sums = [a + b for a, b in zip(own, sums)]
    total, rest = sum_end(0)
    sum_start(1, total, rest)
    sums = gather(work, copies, ORDER[4:], sums)
    powers.append(joined(*sums) * scale)
    total, rest = sum_end(1)
    sum_start(2, total, rest)
    total, rest = sum_end(2)
    total, rest = quick_sum(total, rest)

    def moment(order):
        here = lane_at == lax.rem(row_at, FIELDS) + FIELDS * order
        return tuple(jnp.sum(jnp.where(here, value, 0.0), axis=1, keepdims=True) for value in (total, rest))

    found_by, left_by = coefficients([moment(order) for order in range(6)])

    def mix(factors):
        terms = [factor * power for factor, power in zip(factors, powers)]
        return sum(terms[1:], terms[0])

    found, left = mix(found_by), mix(left_by)
    for block in range(2):
        out_ref[:, 0, block, :] = found[4 * block : 4 * block + 4]
        res_ref[:, 0, block, :] = left[4 * block : 4 * block + 4]

    for copies in all_copies:
        for copy in copies:
            copy.wait_send()
    for stage in range(3):
        sum_all(stage).wait_send()


def solution(mesh):
    n_basin, n_front = mesh.shape["basin"], mesh.shape["front"]
    sizes = (n_basin // 2, n_front // Z_SIZE, Z_SIZE)
    n_xy = sizes[0] * sizes[1]

    def step(right_side, offsets, counts):
        shape = jax.ShapeDtypeStruct(right_side.shape, F32)
        return pl.pallas_call(
            lambda *refs: kernel(sizes, *refs),
            out_shape=(shape, shape),
            in_specs=[pl.BlockSpec(memory_space=pl.ANY)] * 3,
            out_specs=(pl.BlockSpec(memory_space=pltpu.VMEM), pl.BlockSpec(memory_space=pltpu.VMEM)),
            scratch_shapes=[
                pltpu.VMEM(right_side.shape, F32),
                pltpu.VMEM(offsets.shape, F32),
                pltpu.VMEM(counts.shape, jnp.int32),
                pltpu.VMEM((12, 8, POINTS), F32),
                pltpu.VMEM((12, FIELDS, POINTS), F32),
                pltpu.VMEM((12, FIELDS, POINTS), F32),
                pltpu.VMEM((18, POINTS, POINTS), BF16),
                pltpu.VMEM((18, POINTS, POINTS), BF16),
                pltpu.VMEM((3, 128), F32),
                pltpu.VMEM((2, 128), F32),
                pltpu.VMEM((n_xy, 128), F32),
                pltpu.VMEM((Z_SIZE, 128), F32),
                pltpu.SemaphoreType.DMA((3,)),
                pltpu.SemaphoreType.DMA((3, 8)),
                pltpu.SemaphoreType.DMA((3, 8)),
                pltpu.SemaphoreType.DMA((3,)),
                pltpu.SemaphoreType.DMA((3,)),
            ],
            compiler_params=pltpu.CompilerParams(
                collective_id=0, has_side_effects=True, vmem_limit_bytes=48 * 2**20
            ),
        )(right_side, offsets, counts)

    part = P(None, "basin", "front", None)
    return jax.shard_map(
        step, mesh=mesh, in_specs=(part, part, P("basin", "front")), out_specs=(part, part), check_vma=False
    )
```
